32 devices in a mesh: seq: 8 (over z, core), req: 4 (over y, x).
Axes of the slice: x: 2, y: 2, z: 4, core: 2. Of those that a mesh axis runs over, the one named last changes fastest.
Arguments:
- token_ids: int32 [32, 4], replicated, may hold values from 0 to 64127
- embed_table: bfloat16 [64128, 2048], P('req', 'seq'), may hold values from -9 to 9
- cache_len: int32 [32], P('req'), may hold values from 1 to 2048, as said below
- range_start: int32 [32], P('req'), may hold values from 0 to 1023, as said below
- positions: int32 [32], P('req'), may hold values from 0 to 131071
- cached_key_rows: bfloat16 [32, 2048, 512], P('req', 'seq'), may hold values from -220 to 220
- cached_value_rows: bfloat16 [32, 2048, 512], P('req', 'seq'), may hold values from -6 to 6
- attn_gain: bfloat16 [2048], P('seq'), may hold values from 0.099609375 to 1.8984375
- mlp_gain: bfloat16 [2048], P('seq'), may hold values from 0.099609375 to 1.8984375
- w_qkv: bfloat16 [2048, 3072], P('seq'), may hold values from -0.125 to 0.125
- w_out: bfloat16 [2048, 2048], P(None, 'seq'), may hold values from -0.125 to 0.125
- w_gate: bfloat16 [2048, 8192], P('seq', 'req'), may hold values from -0.125 to 0.125
- w_up: bfloat16 [2048, 8192], P('seq', 'req'), may hold values from -0.125 to 0.125
- w_down: bfloat16 [8192, 2048], P('req', 'seq'), may hold values from -0.0625 to 0.0625
Outputs:
- layer_out: bfloat16 [32, 4, 2048], P('req', None, 'seq')
- new_keys: bfloat16 [32, 4, 512], P('req')
- new_values: bfloat16 [32, 4, 512], P('req')
The draws below stay inside these ranges and needn't reach their ends.
Inputs may be any that keep to these rules, and one draw needn't show every extreme that they name: `cache_len`: every request has at least one cached position and some request fills all 2048 positions. A request's range_start is at most (cache_len - 1) // 2 of the same request.
All inputs are finite; a program needn't handle non-finite values.
Results may differ from the reference program's by a relative error of at most 0.02.
Values may be sent and summed in bfloat16 or wider, within the bound.
No kernel may reach another device: no remote copies, remote signals or barrier semaphores. Data moves between devices by JAX's collectives and lax.ppermute only.
A program may use at most 64 MiB of HBM per device.

```python
import math
import jax
import jax.numpy as jnp
import numpy as np
from jax import lax

D = 2048
QUERY_HEADS = 32
KEY_VALUE_HEADS = 8
HEAD_SIZE = 64
FF = 8192
VOCAB = 64128
STEPS = 4
REQUESTS = 32
CTX = 2048
KVW = 512
QKV = 3072


def lengths_pair(key):
    base = jax.random.fold_in(key, 71)
    first_key, order_key, start_key = jax.random.split(base, 3)
    lengths = jax.random.randint(first_key, (REQUESTS,), 1, CTX + 1)
    order = jax.random.permutation(order_key, REQUESTS)
    lengths = lengths.at[order[0]].set(CTX).at[order[1]].set(1)
    starts = jax.random.randint(start_key, (REQUESTS,), 0, (lengths - 1) // 2 + 1)
    starts = starts.at[order[0]].set((CTX - 1) // 2)
    return (lengths.astype(jnp.int32), starts.astype(jnp.int32))


def draw_cache_len(key, part):
    return lengths_pair(key)[0]


def draw_range_start(key, part):
    return lengths_pair(key)[1]


def draw_cached_key_rows(key, part):
    keys = jnp.clip(jax.random.normal(jax.random.fold_in(key, 5), (REQUESTS, CTX, KVW), jnp.float32), -6.0, 6.0)
    return keys.astype(jnp.bfloat16)


def draw_embed_table(key, part):
    columns = jnp.exp(jnp.log(0.6) + jnp.log(3.0) * jnp.arange(D, dtype=jnp.float32) / (D - 1))
    values = jnp.clip(jax.random.normal(jax.random.fold_in(key, 17), (VOCAB, D), jnp.float32), -5.0, 5.0)
    return (values * columns[None, :]).astype(jnp.bfloat16)


def with_ends(entries, own_key, least, top_value):
    spot = [jax.random.randint(jax.random.fold_in(own_key, axis), (), 0, length) for axis, length in enumerate(entries.shape)]
    longest = entries.shape.index(max(entries.shape))
    beside = spot[:longest] + [(spot[longest] + 1) % entries.shape[longest]] + spot[longest + 1:]
    return entries.at[tuple(spot)].set(least).at[tuple(beside)].set(top_value)


def steps_of(key, extent, shards, low, high):
    def one(dim, shards_of):
        heights = jax.random.uniform(jax.random.fold_in(jax.random.fold_in(key, 6), dim), (shards_of,), jnp.float32, low / len(shards), high / len(shards))
        return jnp.repeat(jnp.exp(heights), extent[dim] // shards_of).reshape((-1,) + (1,) * (len(extent) - dim - 1))

    level = one(*shards[0])
    for cut in shards[1:]:
        level = level * one(*cut)
    return level


def rank_table(number_of, lean):
    loads = [(1 << 20) // math.isqrt(rank ** lean) + 1 for rank in range(1, number_of + 1)]
    width = 1 + sum(loads) // (1 << 30)
    return np.cumsum(np.array([max(1, weight // width) for weight in loads]))


def ranked_ids(rng, extent, number_of, skew):
    table = rank_table(number_of, skew)
    pick = jax.random.randint(jax.random.fold_in(rng, 1), extent, 0, int(table[number_of - 1]))
    standing = jnp.searchsorted(jnp.asarray(table, jnp.int32), pick, side="right")
    return jax.random.permutation(jax.random.fold_in(rng, 2), number_of)[standing].astype(jnp.int32)


def normal_values(rng, shape, scale, bound, shards=(), kind=jnp.bfloat16):
    loudness = steps_of(rng, shape, shards, -0.22, 0.18) if shards else 1.0
    entries = jax.random.normal(rng, shape, jnp.float32) * scale * loudness
    return jnp.minimum(jnp.maximum(entries, -bound), bound).astype(kind)


def setup_inputs(seed: int = 0) -> dict:
    arg_keys = jax.random.split(jax.random.key(seed), 15)
    token_ids = with_ends(ranked_ids(arg_keys[0], (REQUESTS, STEPS), VOCAB, 2), jax.random.fold_in(arg_keys[0], 3), 0, VOCAB - 1).astype(jnp.int32)
    embed_table = draw_embed_table(jax.random.fold_in(arg_keys[14], 71), 0)
    cache_len = draw_cache_len(jax.random.fold_in(arg_keys[14], 71), 0)
    range_start = draw_range_start(jax.random.fold_in(arg_keys[14], 71), 0)
    positions = with_ends(jax.random.randint(arg_keys[4], (REQUESTS,), 0, 131072), jax.random.fold_in(arg_keys[4], 1), 0, 131071).astype(jnp.int32)
    cached_key_rows = draw_cached_key_rows(jax.random.fold_in(arg_keys[14], 71), 0)
    cached_value_rows = normal_values(arg_keys[6], (REQUESTS, CTX, KVW), 1.0, 6.0, ((0, 4), (1, 8)))
    attn_gain = jnp.clip(1.0 + 0.18 * jax.random.normal(arg_keys[7], (D,), jnp.float32), 0.099609375, 1.8984375).astype(jnp.bfloat16)
    mlp_gain = jnp.clip(1.0 + 0.18 * jax.random.normal(arg_keys[8], (D,), jnp.float32), 0.099609375, 1.8984375).astype(jnp.bfloat16)
    w_qkv = normal_values(arg_keys[9], (D, QKV), D ** -0.5, 0.125, ((0, 8),))
    w_out = normal_values(arg_keys[10], (QUERY_HEADS * HEAD_SIZE, D), (QUERY_HEADS * HEAD_SIZE) ** -0.5, 0.125, ((1, 8),))
    w_gate = normal_values(arg_keys[11], (D, FF), D ** -0.5, 0.125, ((0, 8), (1, 4)))
    w_up = normal_values(arg_keys[12], (D, FF), D ** -0.5, 0.125, ((0, 8), (1, 4)))
    w_down = normal_values(arg_keys[13], (FF, D), FF ** -0.5, 0.0625, ((0, 4), (1, 8)))
    return {"token_ids": token_ids, "embed_table": embed_table, "cache_len": cache_len, "range_start": range_start, "positions": positions, "cached_key_rows": cached_key_rows, "cached_value_rows": cached_value_rows, "attn_gain": attn_gain, "mlp_gain": mlp_gain, "w_qkv": w_qkv, "w_out": w_out, "w_gate": w_gate, "w_up": w_up, "w_down": w_down}


EPSILON = 1e-05
ROPE_BASE = 500000.0

def rms_scale(values, gain):
    mean_square = lax.optimization_barrier(jnp.mean(values * values, axis=-1, keepdims=True))
    return (values * lax.rsqrt(mean_square + EPSILON) * gain.astype(jnp.float32)).astype(jnp.bfloat16)

def rotary_embedding(vectors, angle_positions):
    half_size = vectors.shape[-1] // 2
    freqs = ROPE_BASE ** (-2.0 * jnp.arange(half_size, dtype=jnp.float32) / vectors.shape[-1])
    angles = angle_positions[:, None] * freqs[None, :]
    cosine = jnp.cos(angles)[:, None, :]
    sine = jnp.sin(angles)[:, None, :]
    first_half = vectors[..., :half_size]
    second_half = vectors[..., half_size:]
    return jnp.concatenate([first_half * cosine - second_half * sine, second_half * cosine + first_half * sine], axis=-1)

def attend_one(inputs):
    query_rows, stored_keys, stored_values, visible, newest_keys, newest_values = inputs
    head_groups = QUERY_HEADS // KEY_VALUE_HEADS
    scale = 1.0 / math.sqrt(HEAD_SIZE)
    query_float = query_rows.astype(jnp.float32).reshape(KEY_VALUE_HEADS, head_groups, HEAD_SIZE)
    key_float = stored_keys.astype(jnp.float32).reshape(-1, KEY_VALUE_HEADS, HEAD_SIZE)
    scores = jnp.einsum('hgd,phd->hgp', query_float, key_float) * scale
    scores = jnp.where(visible[None, None, :], scores, -1e+30)
    newest_query_float = newest_keys.astype(jnp.float32).reshape(-1, KEY_VALUE_HEADS, HEAD_SIZE)
    fresh_scores = jnp.einsum('hgd,jhd->hgj', query_float, newest_query_float) * scale
    top = jnp.maximum(lax.optimization_barrier(jnp.max(scores, axis=-1)), lax.optimization_barrier(jnp.max(fresh_scores, axis=-1)))
    expo = jnp.where(visible[None, None, :], jnp.exp(scores - top[..., None]), 0.0)
    fresh_expo = jnp.exp(fresh_scores - top[..., None])
    total = lax.optimization_barrier(jnp.sum(expo, axis=-1)) + lax.optimization_barrier(jnp.sum(fresh_expo, axis=-1))
    weights = lax.optimization_barrier(expo.astype(jnp.bfloat16)).astype(jnp.float32)
    fresh_weights = lax.optimization_barrier(fresh_expo.astype(jnp.bfloat16)).astype(jnp.float32)
    value_float = stored_values.astype(jnp.float32).reshape(-1, KEY_VALUE_HEADS, HEAD_SIZE)
    newest_value_float = newest_values.astype(jnp.float32).reshape(-1, KEY_VALUE_HEADS, HEAD_SIZE)
    summed = jnp.einsum('hgp,phd->hgd', weights, value_float) + jnp.einsum('hgj,jhd->hgd', fresh_weights, newest_value_float)
    return (summed / total[..., None]).reshape(QUERY_HEADS * HEAD_SIZE).astype(jnp.bfloat16)

def reference(token_ids, embed_table, cache_len, range_start, positions, cached_key_rows, cached_value_rows, attn_gain, mlp_gain, w_qkv, w_out, w_gate, w_up, w_down):
    embedded = embed_table[token_ids]
    request_count = token_ids.shape[0]
    steps = token_ids.shape[1]
    context = cached_key_rows.shape[1]
    key_value_width = KEY_VALUE_HEADS * HEAD_SIZE
    place = jnp.arange(context, dtype=jnp.int32)
    visible = (place[None, :] >= range_start[:, None]) & (place[None, :] < cache_len[:, None])
    key_collection = []
    value_collection = []
    layer_rows = []
    for decode_layer_step in range(steps):
        resid_in = embedded[:, decode_layer_step].astype(jnp.float32)
        normed = rms_scale(resid_in, attn_gain)
        combined_parts = jnp.dot(normed, w_qkv, preferred_element_type=jnp.float32)
        angle_positions = (positions + decode_layer_step).astype(jnp.float32)
        query_rows = rotary_embedding(combined_parts[:, :QUERY_HEADS * HEAD_SIZE].reshape(request_count, QUERY_HEADS, HEAD_SIZE), angle_positions).astype(jnp.bfloat16)
        newest_key_seed = rotary_embedding(combined_parts[:, QUERY_HEADS * HEAD_SIZE:QUERY_HEADS * HEAD_SIZE + key_value_width].reshape(request_count, KEY_VALUE_HEADS, HEAD_SIZE), angle_positions)
        key_collection.append(newest_key_seed.reshape(request_count, key_value_width).astype(jnp.bfloat16))
        value_collection.append(combined_parts[:, QUERY_HEADS * HEAD_SIZE + key_value_width:].astype(jnp.bfloat16))
        newest_key_rows = jnp.stack(key_collection, axis=1)
        newest_value_rows = jnp.stack(value_collection, axis=1)
        attended = lax.map(attend_one, (query_rows, cached_key_rows, cached_value_rows, visible, newest_key_rows, newest_value_rows))
        resid = (resid_in + jnp.dot(attended, w_out, preferred_element_type=jnp.float32)).astype(jnp.bfloat16)
        resid_f = resid.astype(jnp.float32)
        mlp_in = rms_scale(resid_f, mlp_gain)
        gate = jnp.dot(mlp_in, w_gate, preferred_element_type=jnp.float32)
        upper = jnp.dot(mlp_in, w_up, preferred_element_type=jnp.float32)
        hidden = (jax.nn.silu(gate) * upper).astype(jnp.bfloat16)
        layer_rows.append((resid_f + jnp.dot(hidden, w_down, preferred_element_type=jnp.float32)).astype(jnp.bfloat16))
    return (jnp.stack(layer_rows, axis=1), jnp.stack(key_collection, axis=1), jnp.stack(value_collection, axis=1))
```

```python
import functools
import math

import jax
import jax.numpy as jnp
import numpy as np
from jax import lax
from jax.experimental import pallas as pl
from jax.experimental.pallas import tpu as pltpu
from jax.sharding import PartitionSpec as P

D = 2048
QUERY_HEADS = 32
KEY_VALUE_HEADS = 8
HEAD_SIZE = 64
GROUP = QUERY_HEADS // KEY_VALUE_HEADS
EPSILON = 1e-05
ROPE_BASE = 500000.0

HEADS = QUERY_HEADS // 2
KV_HEADS = KEY_VALUE_HEADS // 2
QW = HEADS * HEAD_SIZE
KW = KV_HEADS * HEAD_SIZE
HALF = QW + 2 * KW
LANES = 128
LOW = -1e30

BF16 = jnp.bfloat16
F32 = jnp.float32
SMEM = pl.BlockSpec(memory_space=pltpu.SMEM)
VMEM = pl.BlockSpec(memory_space=pltpu.VMEM)
ANY = pl.BlockSpec(memory_space=pl.ANY)


def mm(a, b):
    return lax.dot_general(a, b, (((1,), (0,)), ((), ())), preferred_element_type=F32)


def mm_t(a, b):
    return lax.dot_general(a, b, (((1,), (1,)), ((), ())), preferred_element_type=F32)


def lane_iota(shape):
    return lax.broadcasted_iota(jnp.int32, shape, len(shape) - 1)


def split(value):
    high = value.astype(BF16).astype(F32)
    low = (value - high).astype(BF16).astype(F32)
    return high, low


def tail_of(value):
    high, low = split(value)
    lane = lane_iota((value.shape[0], LANES))
    return jnp.where(lane == 0, high, jnp.where(lane == 1, low, 0.0))


def tail_sum(*tails):
    total = tails[0].astype(F32)
    for tail in tails[1:]:
        total = total + tail.astype(F32)
    return jnp.sum(total, axis=-1, keepdims=True)


def exchange(array, axis, size, mask):
    return lax.ppermute(array, axis, [(i, i ^ mask) for i in range(size)])


def call(kernel, outs, ins, specs, scratch=(), limit=24, cost=None, name=None):
    return pl.pallas_call(
        kernel,
        out_shape=outs,
        in_specs=specs,
        out_specs=jax.tree.map(lambda _: VMEM, outs),
        scratch_shapes=list(scratch),
        compiler_params=pltpu.CompilerParams(vmem_limit_bytes=limit << 20),
        cost_estimate=cost,
        name=name,
    )(*ins)


def shape(dims, dtype):
    return jax.ShapeDtypeStruct(tuple(dims), dtype)


def lookup_kernel(rows, place, ids_s, ids_v, table, out, blocks, sem):
    req_count, count = out.shape[0], out.shape[1]
    vocab_dev = table.shape[0]
    me = place[2]
    base = me * vocab_dev

    def block_copy(k, j):
        local = ids_s[(me ^ k) * count + j] - base
        inside = (local >= 0) & (local < vocab_dev)
        first = jnp.minimum(lax.div(jnp.clip(local, 0, vocab_dev - 1), rows) * rows, vocab_dev - rows)
        copy = pltpu.make_async_copy(
            table.at[pl.ds(pl.multiple_of(first, 8), rows)], blocks.at[k, j], sem
        )
        return inside, copy

    for k in range(req_count):
        @pl.loop(0, count)
        def _(j):
            inside, copy = block_copy(k, j)
            pl.when(inside)(copy.start)

    for k in range(req_count):
        @pl.loop(0, count)
        def _(j):
            inside, copy = block_copy(k, j)
            pl.when(inside)(copy.wait)

    for k in range(req_count):
        local = ids_v[me ^ k] - base
        inside = (local >= 0) & (local < vocab_dev)
        first = jnp.minimum(lax.div(jnp.clip(local, 0, vocab_dev - 1), rows) * rows, vocab_dev - rows)
        row = jnp.where(inside, local - first, -1)[:, :, None]
        at = lax.broadcasted_iota(jnp.int32, (count, rows, 1), 1)
        taken = jnp.where(at == row, blocks[k].astype(F32), 0.0)
        out[k] = jnp.sum(taken, axis=1).astype(BF16)


def project_kernel(parts, place, gain, weight, *refs):
    blocks, (x_out, keep, give) = refs[:parts], refs[parts:]
    x = blocks[0][...].astype(F32)
    for block in blocks[1:]:
        x = x + block[...].astype(F32)
    x_out[...] = x.astype(BF16)
    scaled = (x * gain[...].astype(F32)).astype(BF16)
    tail = tail_of(jnp.sum(x * x, axis=-1, keepdims=True)).astype(BF16)
    first = place[0] == 0
    q_end, k_end = 2 * QW, 2 * QW + 2 * KW
    at = 0
    for start, width in ((0, QW), (q_end, KW), (k_end, KW)):
        one = mm(scaled, weight[:, start : start + width])
        two = mm(scaled, weight[:, start + width : start + 2 * width])
        keep[:, at : at + width] = jnp.where(first, one, two).astype(BF16)
        give[:, at : at + width] = jnp.where(first, two, one).astype(BF16)
        at += width
    keep[:, HALF:] = tail
    give[:, HALF:] = tail


def add_kernel(a, b, out):
    out[:, :HALF] = (a[:, :HALF].astype(F32) + b[:, :HALF].astype(F32)).astype(BF16)
    out[:, HALF:] = tail_of(tail_sum(a[:, HALF:], b[:, HALF:])).astype(BF16)


def rotate(v, cosine, sine):
    width = v.shape[-1]
    lane = lane_iota(v.shape)
    half = HEAD_SIZE // 2
    ahead = pltpu.roll(v, width - half, 1)
    behind = pltpu.roll(v, half, 1)
    other = jnp.where(lane % HEAD_SIZE < half, ahead, behind)
    reps = width // LANES
    cosine = jnp.concatenate([cosine] * reps, axis=1)
    sine = jnp.concatenate([sine] * reps, axis=1)
    return v * cosine + other * sine


def attend_kernel(
    steps, place, starts, lens, a, b, cosine, sine, fold, keys, keys2, values, values2,
    packed, new_k, new_v, out_rows, stats,
):
    count = a.shape[0]
    requests = count // steps
    rows = steps * HEADS
    context = keys.shape[1]
    core, z, me = place[0], place[1], place[3]
    total = a[:, :HALF].astype(F32) + b[:, :HALF].astype(F32)
    squares = tail_sum(a[:, HALF:], b[:, HALF:])
    total = total * lax.rsqrt(squares / D + EPSILON)
    q = rotate(total[:, :QW], cosine[...], sine[...]).astype(BF16)
    k = rotate(total[:, QW : QW + KW], cosine[...], sine[...]).astype(BF16)
    v = total[:, QW + KW :].astype(BF16)
    new_k[...] = k
    new_v[...] = v

    head = lax.broadcasted_iota(jnp.int32, (count, HEADS, QW), 1)
    lane = lax.broadcasted_iota(jnp.int32, (count, HEADS, QW), 2)
    own_head = lane // HEAD_SIZE == head
    wide = jnp.where(own_head, q.astype(F32)[:, None, :], 0.0).astype(BF16)
    q_rows = mm(wide.reshape(count * HEADS, QW), fold[...]).astype(BF16)

    scale = 1.0 / math.sqrt(HEAD_SIZE)
    fresh_all = mm_t(q_rows, k) * scale
    columns = pl.ds(pl.multiple_of(core * KW, KW), KW)
    spot = lax.broadcasted_iota(jnp.int32, (1, context), 1)
    row_head = lax.broadcasted_iota(jnp.int32, (rows, KW), 0) % HEADS
    own_kv = lane_iota((rows, KW)) // HEAD_SIZE == row_head // GROUP
    row_step = lax.broadcasted_iota(jnp.int32, (rows, count), 0) // HEADS
    fresh_at = lane_iota((rows, count))
    stat_lane = lane_iota((rows, LANES))
    stat_head = lax.broadcasted_iota(jnp.int32, (rows, LANES), 0) % HEADS
    for r in range(requests):
        qr = q_rows[r * rows : (r + 1) * rows]
        lo, hi = starts[r], lens[r]
        place_a = spot + me * context
        place_b = spot + (me ^ 1) * context
        seen_a = (place_a >= lo) & (place_a < hi)
        seen_b = (place_b >= lo) & (place_b < hi)
        seen_f = (fresh_at >= r * steps) & (fresh_at <= r * steps + row_step) & (z == 0)
        sa = jnp.where(seen_a, mm_t(qr, keys[r, :, columns]) * scale, LOW)
        sb = jnp.where(seen_b, mm_t(qr, keys2[r, :, columns]) * scale, LOW)
        sf = jnp.where(seen_f, fresh_all[r * rows : (r + 1) * rows], LOW)
        top = jnp.maximum(
            jnp.maximum(jnp.max(sa, axis=-1, keepdims=True), jnp.max(sb, axis=-1, keepdims=True)),
            jnp.max(sf, axis=-1, keepdims=True),
        )
        top_high, top_low = split(top)
        top = top_high + top_low
        pa = jnp.where(seen_a, jnp.exp(sa - top), 0.0)
        pb = jnp.where(seen_b, jnp.exp(sb - top), 0.0)
        pf = jnp.where(seen_f, jnp.exp(sf - top), 0.0)
        weight = (
            jnp.sum(pa, axis=-1, keepdims=True)
            + jnp.sum(pb, axis=-1, keepdims=True)
            + jnp.sum(pf, axis=-1, keepdims=True)
        )
        o = (
            mm(pa.astype(BF16), values[r, :, columns])
            + mm(pb.astype(BF16), values2[r, :, columns])
            + mm(pf.astype(BF16), v)
        )
        out_rows[r * rows : (r + 1) * rows, :] = jnp.where(own_kv, o, 0.0).astype(BF16)
        w_high, w_low = split(weight)
        stat = jnp.where(stat_lane == stat_head, top_high, 0.0)
        stat = jnp.where(stat_lane == stat_head + HEADS, top_low, stat)
        stat = jnp.where(stat_lane == stat_head + 2 * HEADS, w_high, stat)
        stat = jnp.where(stat_lane == stat_head + 3 * HEADS, w_low, stat)
        stats[r * rows : (r + 1) * rows, :] = stat
    spread = mm_t(out_rows[...], fold[...]).reshape(count, HEADS, QW)
    packed[:, :QW] = jnp.sum(jnp.where(own_head, spread, 0.0), axis=1).astype(BF16)
    packed[:, QW:] = jnp.sum(stats[...].reshape(count, HEADS, LANES), axis=1).astype(BF16)


def read_stats(block):
    block = block.astype(F32)
    both = block + pltpu.roll(block, LANES - HEADS, 1)
    return both, pltpu.roll(both, LANES - 2 * HEADS, 1)


def widen(column_block, spread):
    lane = lane_iota(column_block.shape)
    high, low = split(column_block)
    pair = jnp.where(lane < HEADS, high, jnp.where(lane < 2 * HEADS, pltpu.roll(low, HEADS, 1), 0.0))
    return mm(pair.astype(BF16), spread[...])


def merge(a, b, spread):
    top_a, sum_a = read_stats(a[:, QW:])
    top_b, sum_b = read_stats(b[:, QW:])
    top = jnp.maximum(top_a, top_b)
    fa, fb = jnp.exp(top_a - top), jnp.exp(top_b - top)
    total = sum_a * fa + sum_b * fb
    return top, total, fa, fb


def merge_kernel(a, b, spread, out):
    top, total, fa, fb = merge(a, b, spread)
    wide = widen(fa, spread) * a[:, :QW].astype(F32) + widen(fb, spread) * b[:, :QW].astype(F32)
    out[:, :QW] = wide.astype(BF16)
    lane = lane_iota(top.shape)
    top_high, top_low = split(top)
    w_high, w_low = split(total)
    stat = jnp.where(lane < HEADS, top_high, 0.0)
    stat = jnp.where((lane >= HEADS) & (lane < 2 * HEADS), pltpu.roll(top_low, HEADS, 1), stat)
    stat = jnp.where((lane >= 2 * HEADS) & (lane < 3 * HEADS), pltpu.roll(w_high, 2 * HEADS, 1), stat)
    stat = jnp.where((lane >= 3 * HEADS) & (lane < 4 * HEADS), pltpu.roll(w_low, 3 * HEADS, 1), stat)
    out[:, QW:] = stat.astype(BF16)


def output_kernel(place, a, b, spread, w_own, w_two, out):
    top, total, fa, fb = merge(a, b, spread)
    lane = lane_iota(top.shape)
    total = jnp.where(lane < HEADS, total, 1.0)
    fa, fb = fa / total, fb / total
    wide = widen(fa, spread) * a[:, :QW].astype(F32) + widen(fb, spread) * b[:, :QW].astype(F32)
    attended = wide.astype(BF16)
    core = place[0]
    rows = pl.ds(pl.multiple_of(core * QW, QW), QW)
    own = mm(attended, w_own[rows, :])
    two = mm(attended, w_two[rows, :])
    first = core == 0
    width = own.shape[1]
    out[:, :width] = jnp.where(first, own, two)
    out[:, width:] = jnp.where(first, two, own)


def gate_kernel(parts, place, gains, g_own, g_two, u_own, u_two, *refs):
    blocks, (out, rows_ref) = refs[:parts], refs[parts:]
    count = blocks[0].shape[0]
    for i, block in enumerate(blocks):
        rows_ref[i * count : (i + 1) * count, :] = block[...]
    core, z = place[0], place[1]
    chunks, size = out.shape[0], out.shape[1]
    taken = [
        rows_ref[pl.ds(pl.multiple_of((z ^ j) * size, size), size), :].astype(F32)
        for j in range(chunks)
    ]
    x = jnp.concatenate(taken, axis=0)
    squares = jnp.sum(x * x, axis=-1, keepdims=True)
    scaled = (x * gains[...].astype(F32)).astype(BF16)
    feat = scaled.shape[1] // 2
    first = core == 0
    mine = jnp.where(first, scaled[:, :feat], scaled[:, feat:])
    theirs = jnp.where(first, scaled[:, feat:], scaled[:, :feat])
    hid = g_own.shape[1] // 2
    columns = pl.ds(pl.multiple_of(core * hid, hid), hid)
    gate = mm(mine, g_own[:, columns]) + mm(theirs, g_two[:, columns])
    up = mm(mine, u_own[:, columns]) + mm(theirs, u_two[:, columns])
    tail = tail_of(squares)
    for j in range(chunks):
        at = slice(j * size, (j + 1) * size)
        out[j, :, :hid] = gate[at].astype(BF16)
        out[j, :, hid : 2 * hid] = up[at].astype(BF16)
        out[j, :, 2 * hid :] = tail[at].astype(BF16)


def hidden_kernel(parts, *refs):
    blocks, out = refs[:parts], refs[parts]
    hid = out.shape[1]
    total = blocks[0][:, : 2 * hid].astype(F32)
    for block in blocks[1:]:
        total = total + block[:, : 2 * hid].astype(F32)
    squares = tail_sum(*[block[:, 2 * hid :] for block in blocks])
    inverse = lax.rsqrt(squares / D + EPSILON)
    gate, up = total[:, :hid] * inverse, total[:, hid:] * inverse
    out[...] = (gate / (1.0 + jnp.exp(-gate)) * up).astype(BF16)


def down_kernel(parts, place, w_down, *refs):
    mine, theirs, (out, rows_ref) = refs[:parts], refs[parts : 2 * parts], refs[2 * parts :]
    core, z = place[0], place[1]
    size, hid = mine[0].shape
    near = jnp.concatenate([ref[...] for ref in mine], axis=0)
    far = jnp.concatenate([ref[...] for ref in theirs], axis=0)
    total = mm(near, w_down[pl.ds(pl.multiple_of(core * hid, hid), hid), :]) + mm(
        far, w_down[pl.ds(pl.multiple_of((1 - core) * hid, hid), hid), :]
    )
    for j in range(parts):
        rows_ref[pl.ds(pl.multiple_of((z ^ j) * size, size), size), :] = total[
            j * size : (j + 1) * size
        ]
    count = out.shape[1]
    for k in range(out.shape[0]):
        out[k] = rows_ref[k * count : (k + 1) * count, :].astype(BF16)


def shards(
    seq_size,
    req_size,
    token_ids,
    embed_table,
    cache_len,
    range_start,
    positions,
    cached_key_rows,
    cached_value_rows,
    attn_gain,
    mlp_gain,
    w_qkv,
    w_out,
    w_gate,
    w_up,
    w_down,
):
    requests, steps = cache_len.shape[0], token_ids.shape[1]
    count = requests * steps
    feat = embed_table.shape[1]
    seq_index, req_index = lax.axis_index("seq"), lax.axis_index("req")
    core, z = seq_index % 2, seq_index // 2
    depth = seq_size // 2
    place = jnp.stack([core, z, req_index, seq_index]).astype(jnp.int32)
    swap = lambda array: exchange(array, "seq", seq_size, 1)
    over_z = lambda array, mask: exchange(array, "seq", seq_size, 2 * mask)
    over_req = lambda array, mask: exchange(array, "req", req_size, mask)

    ids = token_ids.reshape(-1)
    rows = 16
    found = call(
        functools.partial(lookup_kernel, rows),
        shape((req_size, count, feat), BF16),
        (place, ids, ids.reshape(req_size, count, 1), embed_table),
        [SMEM, SMEM, VMEM, ANY],
        [pltpu.VMEM((req_size, count, rows, feat), BF16), pltpu.SemaphoreType.DMA],
        name="lookup",
    )
    blocks = [found[0]] + [over_req(found[k], k) for k in range(1, req_size)]

    keys2, values2 = swap(cached_key_rows), swap(cached_value_rows)
    gate2, up2, out2 = swap(w_gate), swap(w_up), swap(w_out)
    gain_two = swap(mlp_gain.reshape(1, feat))
    gain_own = mlp_gain.reshape(1, feat)
    pair = lambda own, two: jnp.where(
        core == 0, jnp.concatenate([own, two], axis=1), jnp.concatenate([two, own], axis=1)
    )

    half = HEAD_SIZE // 2
    freqs = ROPE_BASE ** (-2.0 * jnp.arange(half, dtype=F32) / HEAD_SIZE)
    when = (positions[:, None] + jnp.arange(steps, dtype=jnp.int32)[None, :]).astype(F32)
    angles = when.reshape(count, 1) * freqs[None, :]
    cosine, sine = jnp.cos(angles), jnp.sin(angles)
    cosine = jnp.concatenate([cosine] * 4, axis=1)
    sine = jnp.concatenate([-sine, sine] * 2, axis=1)

    wide = HALF + LANES
    x, keep, give = call(
        functools.partial(project_kernel, req_size),
        (shape((count, feat), BF16), shape((count, wide), BF16), shape((count, wide), BF16)),
        (place, attn_gain.reshape(1, feat), w_qkv, *blocks),
        [SMEM] + [VMEM] * (2 + req_size),
        name="project",
    )
    x_two = swap(x)
    mine, other = keep, swap(give)
    mask = 1
    while mask < depth:
        mine = call(add_kernel, shape((count, wide), BF16), (mine, other), [VMEM] * 2, name="add")
        other = over_z(mine, mask)
        mask *= 2

    head_lane, kv_lane = np.arange(QW)[:, None], np.arange(KW)[None, :]
    fold = jnp.asarray(
        (head_lane % HEAD_SIZE == kv_lane % HEAD_SIZE)
        & (head_lane // (GROUP * HEAD_SIZE) == kv_lane // HEAD_SIZE),
        BF16,
    )
    spread = jnp.asarray(
        (np.arange(LANES)[:, None] % HEADS == np.arange(QW)[None, :] // HEAD_SIZE)
        & (np.arange(LANES)[:, None] < 2 * HEADS),
        BF16,
    )
    packed_width = QW + LANES
    packed, new_k, new_v = call(
        functools.partial(attend_kernel, steps),
        (shape((count, packed_width), BF16), shape((count, KW), BF16), shape((count, KW), BF16)),
        (
            place, range_start, cache_len, mine, other, cosine, sine, fold,
            cached_key_rows, keys2, cached_value_rows, values2,
        ),
        [SMEM] * 3 + [VMEM] * 9,
        [pltpu.VMEM((count * HEADS, KW), BF16), pltpu.VMEM((count * HEADS, LANES), F32)],
        name="attend",
    )
    mine, other, mask = packed, over_z(packed, 1), 2
    while mask < depth:
        mine = call(
            merge_kernel, shape((count, packed_width), BF16), (mine, other, spread), [VMEM] * 3, name="merge"
        )
        other = over_z(mine, mask)
        mask *= 2
    part = call(
        output_kernel,
        shape((count, 2 * feat), F32),
        (place, mine, other, spread, w_out, out2),
        [SMEM] + [VMEM] * 5,
        name="output",
    )
    resid = (pair(x, x_two).astype(F32) + (part + swap(part))).astype(BF16)

    taken = [resid] + [over_req(resid, k) for k in range(1, req_size)]
    gains = pair(gain_own, gain_two)
    size = req_size * count // depth
    hid = w_gate.shape[1] // 2
    terms = call(
        functools.partial(gate_kernel, req_size),
        shape((depth, size, 2 * hid + LANES), BF16),
        (place, gains, w_gate, gate2, w_up, up2, *taken),
        [SMEM] + [VMEM] * (5 + req_size),
        [pltpu.VMEM((req_size * count, 2 * feat), BF16)],
        name="gate",
    )
    sums = [terms[0]] + [over_z(terms[j], j) for j in range(1, depth)]
    hidden = call(
        functools.partial(hidden_kernel, depth),
        shape((size, hid), BF16),
        sums,
        [VMEM] * depth,
        name="hidden",
    )
    near = [hidden] + [over_z(hidden, j) for j in range(1, depth)]
    far = [swap(block) for block in near]
    back = call(
        functools.partial(down_kernel, depth),
        shape((req_size, count, feat), BF16),
        (place, w_down, *near, *far),
        [SMEM] + [VMEM] * (1 + 2 * depth),
        [pltpu.VMEM((req_size * count, feat), F32)],
        name="down",
    )
    total = back[0].astype(F32)
    for k in range(1, req_size):
        total = total + over_req(back[k], k).astype(F32)
    resid_own = lax.dynamic_slice_in_dim(resid, core * feat, feat, axis=1)
    layer_out = (resid_own.astype(F32) + total).astype(BF16)

    new_k2, new_v2 = swap(new_k), swap(new_v)
    return (
        layer_out.reshape(requests, steps, feat),
        pair(new_k, new_k2).reshape(requests, steps, 2 * KW),
        pair(new_v, new_v2).reshape(requests, steps, 2 * KW),
    )


def solution(mesh):
    in_specs = (
        P(),
        P("req", "seq"),
        P("req"),
        P("req"),
        P("req"),
        P("req", "seq", None),
        P("req", "seq", None),
        P("seq"),
        P("seq"),
        P("seq", None),
        P(None, "seq"),
        P("seq", "req"),
        P("seq", "req"),
        P("req", "seq"),
    )
    out_specs = (P("req", None, "seq"), P("req", None, None), P("req", None, None))
    body = functools.partial(shards, mesh.shape["seq"], mesh.shape["req"])
    return jax.shard_map(body, mesh=mesh, in_specs=in_specs, out_specs=out_specs, check_vma=False)
```

```python
import functools
import math

import jax
import jax.numpy as jnp
import numpy as np
from jax import lax
from jax.experimental import pallas as pl
from jax.experimental.pallas import tpu as pltpu
from jax.sharding import PartitionSpec as P

D = 2048
QUERY_HEADS = 32
KEY_VALUE_HEADS = 8
HEAD_SIZE = 64
GROUP = QUERY_HEADS // KEY_VALUE_HEADS
EPSILON = 1e-05
ROPE_BASE = 500000.0

HEADS = QUERY_HEADS // 2
KV_HEADS = KEY_VALUE_HEADS // 2
QW = HEADS * HEAD_SIZE
KW = KV_HEADS * HEAD_SIZE
HALF = QW + 2 * KW
LANES = 128
WIDE = HALF + LANES
LOW = -1e30

BF16 = jnp.bfloat16
F32 = jnp.float32
SMEM = pl.BlockSpec(memory_space=pltpu.SMEM)
VMEM = pl.BlockSpec(memory_space=pltpu.VMEM)
HBM = pl.BlockSpec(memory_space=pltpu.HBM)


def mm(a, b):
    return lax.dot_general(a, b, (((1,), (0,)), ((), ())), preferred_element_type=F32)


def mm_t(a, b):
    return lax.dot_general(a, b, (((1,), (1,)), ((), ())), preferred_element_type=F32)


def lane_iota(shape):
    return lax.broadcasted_iota(jnp.int32, shape, len(shape) - 1)


def split(value):
    high = value.astype(BF16).astype(F32)
    low = (value - high).astype(BF16).astype(F32)
    return high, low


def tail_of(value):
    high, low = split(value)
    lane = lane_iota((value.shape[0], LANES))
    return jnp.where(lane == 0, high, jnp.where(lane == 1, low, 0.0))


def tail_sum(*tails):
    return tree([jnp.sum(tail.astype(F32), axis=-1, keepdims=True) for tail in tails])


def exchange(array, axis, size, mask):
    return lax.ppermute(array, axis, [(i, i ^ mask) for i in range(size)])


WIDE_ORDER, NARROW_ORDER = (3, 1, 2), (2, 1, 3)
LIMIT, LOOKUP_LIMIT, STAGE_LIMIT = 16, 53, 40


def direct(array, size, send, order):
    pick = (lambda k: array[k]) if isinstance(array, list) else (lambda k: array)
    order = [k for k in order if k < size] + [k for k in range(1, size) if k not in order]
    got = {k: send(pick(k), k) for k in order}
    return [pick(0)] + [got[k] for k in range(1, size)]


def call(kernel, outs, ins, specs, scratch=(), limit=LIMIT, cost=None, name=None):
    return pl.pallas_call(
        kernel,
        out_shape=outs,
        in_specs=specs,
        out_specs=jax.tree.map(lambda _: VMEM, outs),
        scratch_shapes=list(scratch),
        compiler_params=pltpu.CompilerParams(vmem_limit_bytes=limit << 20),
        cost_estimate=cost,
        name=name,
    )(*ins)


def work(moved):
    return pl.CostEstimate(flops=0, transcendentals=0, bytes_accessed=moved)


def shape(dims, dtype):
    return jax.ShapeDtypeStruct(tuple(dims), dtype)


def lookup_kernel(rows, place, ids, table, out, blocks, taken, listed, sem):
    req_count, count = out.shape[0], out.shape[1]
    steps = ids.shape[0]
    vocab_dev, feat = table.shape
    me = place[2]
    base = me * vocab_dev
    found = jnp.int32(0)
    for j in range(req_count * count):
        local = ids[j % steps, j // steps] - base
        listed[0, found] = j
        listed[1, found] = local
        found = found + ((local >= 0) & (local < vocab_dev)).astype(jnp.int32)

    def block_of(i):
        local = listed[1, i]
        first = jnp.minimum(local & -rows, vocab_dev - rows)
        return local - first, pltpu.make_async_copy(
            table.at[pl.ds(pl.multiple_of(first, 8), rows)], blocks.at[i], sem
        )

    @pl.loop(0, found)
    def _(i):
        block_of(i)[1].start()

    taken[...] = jnp.zeros(taken.shape, F32)
    at = lax.broadcasted_iota(jnp.int32, (rows, feat), 0)

    @pl.loop(0, found)
    def _(i):
        block_of(i)[1].wait()

    total = req_count * count
    batch = 8

    @pl.loop(0, lax.div(found + batch - 1, batch))
    def _(b):
        for u in range(batch):
            i = b * batch + u
            live = i < found
            j = jnp.where(live, listed[0, i], 0)
            local = jnp.where(live, listed[1, i], 0)
            row = jnp.where(live, local - jnp.minimum(local & -rows, vocab_dev - rows), -1)
            group = lax.div(j, count)
            to = jnp.where(live, (group ^ me) * count + (j - group * count), total)
            picked = jnp.where(at == row, blocks[i].astype(F32), 0.0)
            taken[pl.ds(to, 1), :] = jnp.sum(picked, axis=0, keepdims=True)

    out[...] = taken[:total, :].astype(BF16).reshape(out.shape)


def tables_kernel(when, cosine, sine):
    half = HEAD_SIZE // 2
    lane = lane_iota(cosine.shape)
    freqs = jnp.exp((lane % half).astype(F32) * (-2.0 / HEAD_SIZE * math.log(ROPE_BASE)))
    angles = when[...] * freqs
    cosine[...] = jnp.cos(angles)
    sine[...] = jnp.where(lane % HEAD_SIZE < half, -1.0, 1.0) * jnp.sin(angles)


def run_copies(copies, sems):
    copies = [pltpu.make_async_copy(a, b, sems.at[i]) for i, (a, b) in enumerate(copies)]
    for copy in copies:
        copy.start()
    for copy in copies:
        copy.wait()


def stage_cache_kernel(place, keys, keys2, values, values2, k_out, v_out, sems):
    requests, context = keys.shape[0], keys.shape[1]
    columns = pl.ds(pl.multiple_of(place[0] * KW, KW), KW)
    run_copies(
        [
            (array.at[r, :, columns], out.at[r, pl.ds(i * context, context), :])
            for r in range(requests)
            for out, arrays in ((k_out, (keys, keys2)), (v_out, (values, values2)))
            for i, array in enumerate(arrays)
        ],
        sems,
    )


def stage_gate_kernel(place, g_own, g_two, u_own, u_two, g_out, u_out, sems):
    feat, hid = g_own.shape[0], g_out.shape[1]
    columns = pl.ds(pl.multiple_of(place[0] * hid, LANES), hid)
    pieces = 4
    part = feat // pieces
    run_copies(
        [
            (array.at[pl.ds(p * part, part), columns], out.at[pl.ds(to * feat + p * part, part), :])
            for out, arrays in ((g_out, (g_own, g_two)), (u_out, (u_own, u_two)))
            for array, to in zip(arrays, (place[0], 1 - place[0]))
            for p in range(pieces)
        ],
        sems,
    )


def stage_out_kernel(place, o_own, o_two, k, v, kv_two, o_out, k_out, v_out, sems):
    feat = o_own.shape[1]
    pieces = 4
    part = QW // pieces
    copies = [
        pltpu.make_async_copy(
            array.at[pl.ds(pl.multiple_of(place[0] * QW + p * part, part), part), :],
            o_out.at[pl.ds(p * part, part), pl.ds(pl.multiple_of(to * feat, LANES), feat)],
            sems.at[i * pieces + p],
        )
        for i, (array, to) in enumerate(((o_own, place[0]), (o_two, 1 - place[0])))
        for p in range(pieces)
    ]
    for copy in copies:
        copy.start()
    first = place[0] == 0
    for out, own, two in ((k_out, k, kv_two[:, :KW]), (v_out, v, kv_two[:, KW:])):
        own = own[...]
        pair = jnp.concatenate([jnp.where(first, own, two), jnp.where(first, two, own)], axis=1)
        out[...] = pair.reshape(out.shape)
    for copy in copies:
        copy.wait()


def project_kernel(parts, place, gain, next_gain, weight, *refs):
    blocks, (x_out, keep, give) = refs[:parts], refs[parts:]
    x = blocks[0][...].astype(F32)
    for block in blocks[1:]:
        x = x + block[...].astype(F32)
    x_out[...] = x.astype(BF16)
    scaled = (x * gain[...].astype(F32)).astype(BF16)
    tail = tail_of(jnp.sum(x * x, axis=-1, keepdims=True)).astype(BF16)
    first = place[0] == 0
    q_end, k_end = 2 * QW, 2 * QW + 2 * KW
    at = 0
    for start, width in ((0, QW), (q_end, KW), (k_end, KW)):
        one = mm(scaled, weight[:, start : start + width])
        two = mm(scaled, weight[:, start + width : start + 2 * width])
        keep[:, at : at + width] = jnp.where(first, one, two).astype(BF16)
        give[:, at : at + width] = jnp.where(first, two, one).astype(BF16)
        at += width
    keep[:, HALF:] = tail
    give[:, HALF:WIDE] = tail
    feat = x.shape[1]
    give[:, WIDE : WIDE + feat] = x.astype(BF16)
    give[:, WIDE + feat :] = jnp.broadcast_to(next_gain[...], x.shape)


def tree(values):
    while len(values) > 1:
        values = [values[i] + values[i + 1] for i in range(0, len(values), 2)]
    return values[0]


def add_kernel(a, b, out):
    out[:, :HALF] = (a[:, :HALF].astype(F32) + b[:, :HALF].astype(F32)).astype(BF16)
    out[:, HALF:] = tail_of(tail_sum(a[:, HALF:], b[:, HALF:WIDE])).astype(BF16)


def rotate(v, cosine, sine):
    width = v.shape[-1]
    lane = lane_iota(v.shape)
    half = HEAD_SIZE // 2
    ahead = pltpu.roll(v, width - half, 1)
    behind = pltpu.roll(v, half, 1)
    other = jnp.where(lane % HEAD_SIZE < half, ahead, behind)
    reps = width // LANES
    cosine = jnp.concatenate([cosine] * reps, axis=1)
    sine = jnp.concatenate([sine] * reps, axis=1)
    return v * cosine + other * sine


def attend_kernel(
    steps, parts, place, starts, lens, cosine, sine, fold, keys, values, *refs
):
    sums, (packed, new_k, new_v, out_rows, stats) = refs[:parts], refs[parts:]
    count = packed.shape[0]
    requests = count // steps
    rows = steps * HEADS
    context = keys.shape[1] // 2
    z, me = place[1], place[3]
    total = tree([block[:, :HALF].astype(F32) for block in sums])
    squares = tail_sum(*[block[:, HALF:] for block in sums])
    total = total * lax.rsqrt(squares / D + EPSILON)
    q = rotate(total[:, :QW], cosine[...], sine[...]).astype(BF16)
    k = rotate(total[:, QW : QW + KW], cosine[...], sine[...]).astype(BF16)
    v = total[:, QW + KW :].astype(BF16)
    new_k[...] = k
    new_v[...] = v

    head = lax.broadcasted_iota(jnp.int32, (count, HEADS, QW), 1)
    lane = lax.broadcasted_iota(jnp.int32, (count, HEADS, QW), 2)
    own_head = lane // HEAD_SIZE == head
    wide = jnp.where(own_head, q.astype(F32)[:, None, :], 0.0).astype(BF16)
    q_rows = mm(wide.reshape(count * HEADS, QW), fold[...]).astype(BF16)

    scale = 1.0 / math.sqrt(HEAD_SIZE)
    fresh_all = mm_t(q_rows, k) * scale
    spot = lax.broadcasted_iota(jnp.int32, (1, 2 * context), 1)
    spot = jnp.where(spot < context, spot + me * context, spot - context + (me ^ 1) * context)
    row_head = lax.broadcasted_iota(jnp.int32, (rows, KW), 0) % HEADS
    own_kv = lane_iota((rows, KW)) // HEAD_SIZE == row_head // GROUP
    row_step = lax.broadcasted_iota(jnp.int32, (rows, count), 0) // HEADS
    fresh_at = lane_iota((rows, count))
    stat_lane = lane_iota((rows, LANES))
    stat_head = lax.broadcasted_iota(jnp.int32, (rows, LANES), 0) % HEADS
    for r in range(requests):
        qr = q_rows[r * rows : (r + 1) * rows]
        lo, hi = starts[r], lens[r]
        seen = (spot >= lo) & (spot < hi)
        seen_f = (fresh_at >= r * steps) & (fresh_at <= r * steps + row_step) & (z == 0)
        sc = jnp.where(seen, mm_t(qr, keys[r]) * scale, LOW)
        sf = jnp.where(seen_f, fresh_all[r * rows : (r + 1) * rows], LOW)
        top = jnp.maximum(jnp.max(sc, axis=-1, keepdims=True), jnp.max(sf, axis=-1, keepdims=True))
        top_high, top_low = split(top)
        top = top_high + top_low
        pc = jnp.where(seen, jnp.exp(sc - top), 0.0)
        pf = jnp.where(seen_f, jnp.exp(sf - top), 0.0)
        weight = jnp.sum(pc, axis=-1, keepdims=True) + jnp.sum(pf, axis=-1, keepdims=True)
        o = mm(pc.astype(BF16), values[r]) + mm(pf.astype(BF16), v)
        out_rows[r * rows : (r + 1) * rows, :] = jnp.where(own_kv, o, 0.0).astype(BF16)
        w_high, w_low = split(weight)
        stat = jnp.where(stat_lane == stat_head, top_high, 0.0)
        stat = jnp.where(stat_lane == stat_head + HEADS, top_low, stat)
        stat = jnp.where(stat_lane == stat_head + 2 * HEADS, w_high, stat)
        stat = jnp.where(stat_lane == stat_head + 3 * HEADS, w_low, stat)
        stats[r * rows : (r + 1) * rows, :] = stat
    spread = mm_t(out_rows[...], fold[...]).reshape(count, HEADS, QW)
    packed[:, :QW] = jnp.sum(jnp.where(own_head, spread, 0.0), axis=1).astype(BF16)
    packed[:, QW:] = jnp.sum(stats[...].reshape(count, HEADS, LANES), axis=1).astype(BF16)


def read_stats(block):
    block = block.astype(F32)
    both = block + pltpu.roll(block, LANES - HEADS, 1)
    return both, pltpu.roll(both, LANES - 2 * HEADS, 1)


def widen(column_block, spread):
    lane = lane_iota(column_block.shape)
    high, low = split(column_block)
    pair = jnp.where(lane < HEADS, high, jnp.where(lane < 2 * HEADS, pltpu.roll(low, HEADS, 1), 0.0))
    return mm(pair.astype(BF16), spread[...])


def output_kernel(parts, spread, weight, *refs):
    blocks, out = refs[:parts], refs[parts]
    stats = [read_stats(block[:, QW:]) for block in blocks]
    top = functools.reduce(jnp.maximum, [stat[0] for stat in stats])
    factors = [jnp.exp(stat[0] - top) for stat in stats]
    total = sum(stat[1] * factor for stat, factor in zip(stats, factors))
    inverse = 1.0 / jnp.where(lane_iota(top.shape) < HEADS, total, 1.0)
    wide = sum(
        widen(factor * inverse, spread) * block[:, :QW].astype(F32)
        for factor, block in zip(factors, blocks)
    )
    out[...] = mm(wide.astype(BF16), weight[...])


def gate_kernel(parts, place, gains, w_gate, w_up, *refs):
    blocks, (out, rows_ref) = refs[:parts], refs[parts:]
    count = blocks[0].shape[0]
    for i, block in enumerate(blocks):
        rows_ref[i * count : (i + 1) * count, :] = block[...]
    z = place[1]
    chunks, size = out.shape[0], out.shape[1]
    taken = [
        rows_ref[pl.ds(pl.multiple_of((z ^ j) * size, size), size), :].astype(F32)
        for j in range(chunks)
    ]
    x = jnp.concatenate(taken, axis=0)
    squares = jnp.sum(x * x, axis=-1, keepdims=True)
    scaled = (x * gains[...].astype(F32)).astype(BF16)
    hid = w_gate.shape[1]
    gate, up = mm(scaled, w_gate[...]), mm(scaled, w_up[...])
    tail = tail_of(squares)
    for j in range(chunks):
        at = slice(j * size, (j + 1) * size)
        out[j, :, :hid] = gate[at].astype(BF16)
        out[j, :, hid : 2 * hid] = up[at].astype(BF16)
        out[j, :, 2 * hid :] = tail[at].astype(BF16)


def hidden_kernel(parts, *refs):
    blocks, out = refs[:parts], refs[parts]
    hid = out.shape[1]
    total = blocks[0][:, : 2 * hid].astype(F32)
    for block in blocks[1:]:
        total = total + block[:, : 2 * hid].astype(F32)
    squares = tail_sum(*[block[:, 2 * hid :] for block in blocks])
    inverse = lax.rsqrt(squares / D + EPSILON)
    gate, up = total[:, :hid] * inverse, total[:, hid:] * inverse
    out[...] = (gate / (1.0 + jnp.exp(-gate)) * up).astype(BF16)


def down_kernel(parts, place, w_down, *refs):
    mine, theirs, (out, rows_ref) = refs[:parts], refs[parts : 2 * parts], refs[2 * parts :]
    core, z = place[0], place[1]
    size, hid = mine[0].shape
    near = jnp.concatenate([ref[...] for ref in mine], axis=0)
    far = jnp.concatenate([ref[...] for ref in theirs], axis=0)
    total = mm(near, w_down[pl.ds(pl.multiple_of(core * hid, hid), hid), :]) + mm(
        far, w_down[pl.ds(pl.multiple_of((1 - core) * hid, hid), hid), :]
    )
    for j in range(parts):
        rows_ref[pl.ds(pl.multiple_of((z ^ j) * size, size), size), :] = total[
            j * size : (j + 1) * size
        ]
    count = out.shape[1]
    for k in range(out.shape[0]):
        out[k] = rows_ref[k * count : (k + 1) * count, :].astype(BF16)


def shards(
    seq_size,
    req_size,
    token_ids,
    embed_table,
    cache_len,
    range_start,
    positions,
    cached_key_rows,
    cached_value_rows,
    attn_gain,
    mlp_gain,
    w_qkv,
    w_out,
    w_gate,
    w_up,
    w_down,
):
    requests, steps = cache_len.shape[0], token_ids.shape[1]
    count = requests * steps
    feat = embed_table.shape[1]
    seq_index, req_index = lax.axis_index("seq"), lax.axis_index("req")
    core, z = seq_index % 2, seq_index // 2
    depth = seq_size // 2
    place = jnp.stack([core, z, req_index, seq_index]).astype(jnp.int32)
    swap = lambda array: exchange(array, "seq", seq_size, 1)
    over_z = lambda array, mask: exchange(array, "seq", seq_size, 2 * mask)
    over_req = lambda array, mask: exchange(array, "req", req_size, mask)

    rows = 16
    found = call(
        functools.partial(lookup_kernel, rows),
        shape((req_size, count, feat), BF16),
        (place, token_ids.T, embed_table),
        [SMEM, SMEM, HBM],
        [
            pltpu.VMEM((req_size * count, rows, feat), BF16),
            pltpu.VMEM((req_size * count + 8, feat), F32),
            pltpu.SMEM((2, req_size * count + 1), jnp.int32),
            pltpu.SemaphoreType.DMA,
        ],
        limit=LOOKUP_LIMIT,
        name="lookup",
    )
    blocks = [found[0]] + [over_req(found[k], k) for k in range(1, req_size)]

    hid = w_gate.shape[1] // 2
    context = cached_key_rows.shape[1]
    keys2, values2 = swap(cached_key_rows), swap(cached_value_rows)
    *blocks, keys2, values2 = lax.optimization_barrier((*blocks, keys2, values2))
    next_gain = mlp_gain.reshape(1, feat)
    when = (positions[:, None] + jnp.arange(steps, dtype=jnp.int32)[None, :]).astype(F32)
    cosine, sine = call(
        tables_kernel,
        (shape((count, LANES), F32),) * 2,
        (when.reshape(count, 1),),
        [VMEM],
        cost=work(1 << 20),
        name="tables",
    )

    x, keep, give = call(
        functools.partial(project_kernel, req_size),
        (
            shape((count, feat), BF16),
            shape((count, WIDE), BF16),
            shape((count, WIDE + 2 * feat), BF16),
        ),
        (place, attn_gain.reshape(1, feat), next_gain, w_qkv, *blocks),
        [SMEM] + [VMEM] * (3 + req_size),
        name="project",
    )
    got = swap(give)
    mine = call(add_kernel, shape((count, WIDE), BF16), (keep, got), [VMEM] * 2, name="add")
    sums = direct(mine, depth, over_z, WIDE_ORDER)
    _, w_gate, w_up = lax.optimization_barrier((mine, w_gate, w_up))
    gate2, up2 = swap(w_gate), swap(w_up)
    keys, values = call(
        stage_cache_kernel,
        (shape((requests, 2 * context, KW), BF16),) * 2,
        (place, cached_key_rows, keys2, cached_value_rows, values2),
        [SMEM] + [HBM] * 4,
        [pltpu.SemaphoreType.DMA((4 * requests,))],
        cost=work(8 * requests * context * KW * 2),
        limit=STAGE_LIMIT,
        name="stage_cache",
    )
    *sums, keys, values, gate2, up2 = lax.optimization_barrier((*sums, keys, values, gate2, up2))

    head_lane, kv_lane = np.arange(QW)[:, None], np.arange(KW)[None, :]
    fold = jnp.asarray(
        (head_lane % HEAD_SIZE == kv_lane % HEAD_SIZE)
        & (head_lane // (GROUP * HEAD_SIZE) == kv_lane // HEAD_SIZE),
        BF16,
    )
    spread = jnp.asarray(
        (np.arange(LANES)[:, None] % HEADS == np.arange(QW)[None, :] // HEAD_SIZE)
        & (np.arange(LANES)[:, None] < 2 * HEADS),
        BF16,
    )
    packed_width = QW + LANES
    packed, new_k, new_v = call(
        functools.partial(attend_kernel, steps, depth),
        (shape((count, packed_width), BF16), shape((count, KW), BF16), shape((count, KW), BF16)),
        (place, range_start, cache_len, cosine, sine, fold, keys, values, *sums),
        [SMEM] * 3 + [VMEM] * (5 + depth),
        [pltpu.VMEM((count * HEADS, KW), BF16), pltpu.VMEM((count * HEADS, LANES), F32)],
        name="attend",
    )
    partials = direct(packed, depth, over_z, NARROW_ORDER)
    _, w_out, new_k, new_v = lax.optimization_barrier((packed, w_out, new_k, new_v))
    o_pair, all_k, all_v = call(
        stage_out_kernel,
        (shape((QW, 2 * feat), BF16),) + (shape((requests, steps, 2 * KW), BF16),) * 2,
        (place, w_out, swap(w_out), new_k, new_v, swap(jnp.concatenate([new_k, new_v], axis=1))),
        [SMEM] + [HBM] * 2 + [VMEM] * 3,
        [pltpu.SemaphoreType.DMA((8,))],
        cost=work(4 * feat * QW * 2),
        limit=STAGE_LIMIT,
        name="stage_out",
    )
    g_pair, u_pair = call(
        stage_gate_kernel,
        (shape((2 * feat, hid), BF16),) * 2,
        (place, w_gate, gate2, w_up, up2),
        [SMEM] + [HBM] * 4,
        [pltpu.SemaphoreType.DMA((16,))],
        cost=work(8 * feat * hid * 2),
        limit=STAGE_LIMIT,
        name="stage_gate",
    )
    *partials, o_pair, g_pair, u_pair = lax.optimization_barrier((*partials, o_pair, g_pair, u_pair))
    part = call(
        functools.partial(output_kernel, depth),
        shape((count, 2 * feat), F32),
        (spread, o_pair, *partials),
        [VMEM] * (2 + depth),
        name="output",
    )
    pair = lambda own, two: jnp.where(
        core == 0, jnp.concatenate([own, two], axis=1), jnp.concatenate([two, own], axis=1)
    )
    x_pair = pair(x, got[:, WIDE : WIDE + feat])
    gain_pair = pair(next_gain, got[0:1, WIDE + feat :])
    resid = (x_pair.astype(F32) + (part + swap(part))).astype(BF16)

    taken = direct(resid, req_size, over_req, ())
    size = req_size * count // depth
    terms = call(
        functools.partial(gate_kernel, req_size),
        shape((depth, size, 2 * hid + LANES), BF16),
        (place, gain_pair, g_pair, u_pair, *taken),
        [SMEM] + [VMEM] * (3 + req_size),
        [pltpu.VMEM((req_size * count, 2 * feat), BF16)],
        name="gate",
    )
    sums = direct([terms[j] for j in range(depth)], depth, over_z, WIDE_ORDER)
    hidden = call(
        functools.partial(hidden_kernel, depth),
        shape((size, hid), BF16),
        sums,
        [VMEM] * depth,
        name="hidden",
    )
    near = direct(hidden, depth, over_z, NARROW_ORDER)
    far = [swap(block) for block in near]
    back = call(
        functools.partial(down_kernel, depth),
        shape((req_size, count, feat), BF16),
        (place, w_down, *near, *far),
        [SMEM] + [VMEM] * (1 + 2 * depth),
        [pltpu.VMEM((req_size * count, feat), F32)],
        name="down",
    )
    total = sum(
        block.astype(F32)
        for block in direct([back[k] for k in range(req_size)], req_size, over_req, ())
    )
    resid_own = lax.dynamic_slice_in_dim(resid, core * feat, feat, axis=1)
    layer_out = (resid_own.astype(F32) + total).astype(BF16).reshape(requests, steps, feat)
    return layer_out, all_k, all_v


def solution(mesh):
    in_specs = (
        P(),
        P("req", "seq"),
        P("req"),
        P("req"),
        P("req"),
        P("req", "seq", None),
        P("req", "seq", None),
        P("seq"),
        P("seq"),
        P("seq", None),
        P(None, "seq"),
        P("seq", "req"),
        P("seq", "req"),
        P("req", "seq"),
    )
    out_specs = (P("req", None, "seq"), P("req", None, None), P("req", None, None))
    body = functools.partial(shards, mesh.shape["seq"], mesh.shape["req"])
    return jax.shard_map(body, mesh=mesh, in_specs=in_specs, out_specs=out_specs, check_vma=False)
```

```python
import functools
import math

import jax
import jax.numpy as jnp
import numpy as np
from jax import lax
from jax.experimental import pallas as pl
from jax.experimental.pallas import tpu as pltpu
from jax.sharding import PartitionSpec as P

D = 2048
QUERY_HEADS = 32
KEY_VALUE_HEADS = 8
HEAD_SIZE = 64
GROUP = QUERY_HEADS // KEY_VALUE_HEADS
EPSILON = 1e-05
ROPE_BASE = 500000.0

HEADS = QUERY_HEADS // 2
KV_HEADS = KEY_VALUE_HEADS // 2
QW = HEADS * HEAD_SIZE
KW = KV_HEADS * HEAD_SIZE
HALF = QW + 2 * KW
LANES = 128
TILE = 256
WIDE = HALF + LANES
LOW = -1e30

BF16 = jnp.bfloat16
F32 = jnp.float32
SMEM = pl.BlockSpec(memory_space=pltpu.SMEM)
VMEM = pl.BlockSpec(memory_space=pltpu.VMEM)
HBM = pl.BlockSpec(memory_space=pltpu.HBM)


def mm(a, b):
    return lax.dot_general(a, b, (((1,), (0,)), ((), ())), preferred_element_type=F32)


def mm_t(a, b):
    return lax.dot_general(a, b, (((1,), (1,)), ((), ())), preferred_element_type=F32)


def lane_iota(shape):
    return lax.broadcasted_iota(jnp.int32, shape, len(shape) - 1)


def split(value):
    high = value.astype(BF16).astype(F32)
    low = (value - high).astype(BF16).astype(F32)
    return high, low


def tail_of(value):
    high, low = split(value)
    lane = lane_iota((value.shape[0], LANES))
    return jnp.where(lane == 0, high, jnp.where(lane == 1, low, 0.0))


def tail_sum(*tails):
    return tree([jnp.sum(tail.astype(F32), axis=-1, keepdims=True) for tail in tails])


def exchange(array, axis, size, mask):
    return lax.ppermute(array, axis, [(i, i ^ mask) for i in range(size)])


WIDE_ORDER, NARROW_ORDER, REQ_ORDER = (3, 1, 2), (3, 1, 2), (3, 2, 1)
LIMIT, LOOKUP_LIMIT, STAGE_LIMIT = 12, 53, 48


def direct(array, size, send, order):
    pick = (lambda k: array[k]) if isinstance(array, list) else (lambda k: array)
    order = [k for k in order if k < size] + [k for k in range(1, size) if k not in order]
    got = lax.optimization_barrier(tuple(send(pick(k), k) for k in order))
    return [pick(0)] + [got[order.index(k)] for k in range(1, size)]


def call(kernel, outs, ins, specs, scratch=(), limit=LIMIT, cost=None, name=None):
    return pl.pallas_call(
        kernel,
        out_shape=outs,
        in_specs=specs,
        out_specs=jax.tree.map(lambda _: VMEM, outs),
        scratch_shapes=list(scratch),
        compiler_params=pltpu.CompilerParams(vmem_limit_bytes=limit << 20),
        cost_estimate=cost,
        name=name,
    )(*ins)


def work(moved):
    return pl.CostEstimate(flops=0, transcendentals=0, bytes_accessed=moved)


def time_of(moved):
    return pl.CostEstimate(flops=256 * moved, transcendentals=0, bytes_accessed=0)


def here():
    seq, req = lax.axis_index("seq"), lax.axis_index("req")
    return seq & 1, seq >> 1, req, seq


def shape(dims, dtype):
    return jax.ShapeDtypeStruct(tuple(dims), dtype)


def lookup_kernel(rows, ids, table, out, blocks, taken, listed, sem):
    req_count, count = out.shape[0], out.shape[1]
    steps = ids.shape[0]
    vocab_dev, feat = table.shape
    me = here()[2]
    base = me * vocab_dev
    found = jnp.int32(0)
    for j in range(req_count * count):
        local = ids[j % steps, j // steps] - base
        listed[0, found] = j
        listed[1, found] = local
        found = found + ((local >= 0) & (local < vocab_dev)).astype(jnp.int32)

    def block_of(i):
        local = listed[1, i]
        first = jnp.minimum(local & -rows, vocab_dev - rows)
        return local - first, pltpu.make_async_copy(
            table.at[pl.ds(pl.multiple_of(first, 8), rows)], blocks.at[i], sem
        )

    @pl.loop(0, found)
    def _(i):
        block_of(i)[1].start()

    taken[...] = jnp.zeros(taken.shape, F32)
    at = lax.broadcasted_iota(jnp.int32, (rows, feat), 0)

    @pl.loop(0, found)
    def _(i):
        block_of(i)[1].wait()

    total = req_count * count
    batch = 8

    @pl.loop(0, lax.div(found + batch - 1, batch))
    def _(b):
        for u in range(batch):
            i = b * batch + u
            live = i < found
            j = jnp.where(live, listed[0, i], 0)
            local = jnp.where(live, listed[1, i], 0)
            row = jnp.where(live, local - jnp.minimum(local & -rows, vocab_dev - rows), -1)
            group = lax.div(j, count)
            to = jnp.where(live, (group ^ me) * count + (j - group * count), total)
            picked = jnp.where(at == row, blocks[i].astype(F32), 0.0)
            taken[pl.ds(to, 1), :] = jnp.sum(picked, axis=0, keepdims=True)

    out[...] = taken[:total, :].astype(BF16).reshape(out.shape)


def tables_kernel(starts, lens, when, cosine, sine, bias):
    half = HEAD_SIZE // 2
    lane = lane_iota(cosine.shape)
    freqs = jnp.exp((lane % half).astype(F32) * (-2.0 / HEAD_SIZE * math.log(ROPE_BASE)))
    angles = when[...] * freqs
    cosine[...] = jnp.cos(angles)
    sine[...] = jnp.where(lane % HEAD_SIZE < half, -1.0, 1.0) * jnp.sin(angles)
    me = here()[3]
    context = bias.shape[1] // 2
    spot = lane_iota((1, 2 * context))
    spot = jnp.where(spot < context, spot + me * context, spot - context + (me ^ 1) * context)
    for r in range(bias.shape[0]):
        bias[r : r + 1, :] = jnp.where((spot >= starts[r]) & (spot < lens[r]), 0.0, LOW)


def run_copies(copies, sems):
    copies = [pltpu.make_async_copy(a, b, sems.at[i]) for i, (a, b) in enumerate(copies)]
    for copy in copies:
        copy.start()
    for copy in copies:
        copy.wait()


def stage_cache_kernel(keys, keys2, values, values2, k_out, v_out, sems):
    requests, context = keys.shape[0], keys.shape[1]
    columns = pl.ds(pl.multiple_of(here()[0] * KW, KW), KW)
    run_copies(
        [
            (array.at[r, :, columns], out.at[r, pl.ds(i * context, context), :])
            for r in range(requests)
            for out, arrays in ((k_out, (keys, keys2)), (v_out, (values, values2)))
            for i, array in enumerate(arrays)
        ],
        sems,
    )


def stage_units_kernel(own, two, out, sems):
    feat, hid = own.shape[0], out.shape[1]
    core = here()[0]
    columns = pl.ds(pl.multiple_of(core * hid, LANES), hid)
    pieces = 8
    part = feat // pieces
    run_copies(
        [
            (array.at[pl.ds(p * part, part), columns], out.at[pl.ds(to * feat + p * part, part), :])
            for array, to in ((own, core), (two, 1 - core))
            for p in range(pieces)
        ],
        sems,
    )


def stage_out_kernel(o_own, o_two, out, sems):
    feat = o_own.shape[1]
    core = here()[0]
    pieces = 4
    part = QW // pieces
    run_copies(
        [
            (
                array.at[pl.ds(pl.multiple_of(core * QW + p * part, part), part), :],
                out.at[pl.ds(p * part, part), pl.ds(pl.multiple_of(to * feat, LANES), feat)],
            )
            for array, to in ((o_own, core), (o_two, 1 - core))
            for p in range(pieces)
        ],
        sems,
    )


def join_kernel(k, v, kv_two, k_out, v_out):
    first = here()[0] == 0
    for out, own, two in ((k_out, k, kv_two[:, :KW]), (v_out, v, kv_two[:, KW:])):
        own = own[...]
        pair = jnp.concatenate([jnp.where(first, own, two), jnp.where(first, two, own)], axis=1)
        out[...] = pair.reshape(out.shape)


def project_kernel(parts, gain, next_gain, weight, *refs):
    blocks, (x_out, keep, give) = refs[:parts], refs[parts:]
    x = blocks[0][...].astype(F32)
    for block in blocks[1:]:
        x = x + block[...].astype(F32)
    x_out[...] = x.astype(BF16)
    scaled = (x * gain[...].astype(F32)).astype(BF16)
    tail = tail_of(jnp.sum(x * x, axis=-1, keepdims=True)).astype(BF16)
    first = here()[0] == 0
    q_end, k_end = 2 * QW, 2 * QW + 2 * KW
    at = 0
    for start, width in ((0, QW), (q_end, KW), (k_end, KW)):
        for tile in range(start, start + width, TILE):
            one = mm(scaled, weight[:, tile : tile + TILE]).astype(BF16)
            two = mm(scaled, weight[:, tile + width : tile + width + TILE]).astype(BF16)
            keep[:, at : at + TILE] = jnp.where(first, one, two)
            give[:, at : at + TILE] = jnp.where(first, two, one)
            at += TILE
    keep[:, HALF:] = tail
    give[:, HALF:WIDE] = tail
    feat = x.shape[1]
    give[:, WIDE : WIDE + feat] = x.astype(BF16)
    give[:, WIDE + feat :] = jnp.broadcast_to(next_gain[...], x.shape)


def tree(values):
    while len(values) > 1:
        values = [values[i] + values[i + 1] for i in range(0, len(values), 2)]
    return values[0]


def add_kernel(a, b, out):
    out[:, :HALF] = (a[:, :HALF].astype(F32) + b[:, :HALF].astype(F32)).astype(BF16)
    out[:, HALF:] = tail_of(tail_sum(a[:, HALF:], b[:, HALF:WIDE])).astype(BF16)


def rotate(v, cosine, sine):
    width = v.shape[-1]
    lane = lane_iota(v.shape)
    half = HEAD_SIZE // 2
    ahead = pltpu.roll(v, width - half, 1)
    behind = pltpu.roll(v, half, 1)
    other = jnp.where(lane % HEAD_SIZE < half, ahead, behind)
    reps = width // LANES
    cosine = jnp.concatenate([cosine] * reps, axis=1)
    sine = jnp.concatenate([sine] * reps, axis=1)
    return v * cosine + other * sine


def attend_kernel(steps, parts, cosine, sine, bias, keys, values, *refs):
    sums, (packed, new_k, new_v, q_rows, o_rows, tops, totals) = refs[:parts], refs[parts:]
    count = packed.shape[0]
    requests = count // steps
    rows = steps * HEADS
    z = here()[1]
    total = tree([block[:, :HALF].astype(F32) for block in sums])
    squares = tail_sum(*[block[:, HALF:] for block in sums])
    total = total * lax.rsqrt(squares / D + EPSILON)
    q = rotate(total[:, :QW], cosine[...], sine[...]).astype(BF16)
    k = rotate(total[:, QW : QW + KW], cosine[...], sine[...]).astype(BF16)
    v = total[:, QW + KW :].astype(BF16)
    new_k[...] = k
    new_v[...] = v

    q = q.astype(F32) * (1.0 / math.sqrt(HEAD_SIZE))
    lane = lane_iota((count, LANES))
    per = LANES // HEAD_SIZE
    q_rows[...] = jnp.zeros(q_rows.shape, F32)

    def column(index):
        return slice(index // per * LANES, index // per * LANES + LANES)

    def move(block, at, to):
        return block if at % per == to % per else pltpu.roll(block, HEAD_SIZE, 1)

    for h in range(HEADS):
        kv = h // GROUP
        block = move(q[:, column(h)], h, kv)
        block = jnp.where(lane // HEAD_SIZE == kv % per, block, 0.0)
        q_rows[kv // per, pl.ds(h, count, stride=HEADS), :] = block

    row_step = lax.broadcasted_iota(jnp.int32, (rows, count), 0) // HEADS
    fresh_at = lane_iota((rows, count))
    ats = [slice(r * rows, (r + 1) * rows) for r in range(requests)]
    q_all = [
        jnp.concatenate([q_rows[i, at, :] for i in range(KW // LANES)], axis=1).astype(BF16)
        for at in ats
    ]
    fresh = mm_t(jnp.concatenate(q_all, axis=0), k)
    raw = [mm_t(q_all[r], keys[r]) for r in range(requests)]
    weights = []
    for r, at in enumerate(ats):
        seen_f = (fresh_at >= r * steps) & (fresh_at <= r * steps + row_step) & (z == 0)
        sc = raw[r] + bias[r : r + 1, :]
        sf = jnp.where(seen_f, fresh[at], LOW)
        top = jnp.maximum(jnp.max(sc, axis=-1, keepdims=True), jnp.max(sf, axis=-1, keepdims=True))
        top_high, top_low = split(jnp.maximum(top, LOW / 2))
        top = top_high + top_low
        pc = jnp.exp(sc - top)
        pf = jnp.exp(sf - top)
        weight = jnp.sum(pc, axis=-1, keepdims=True) + jnp.sum(pf, axis=-1, keepdims=True)
        tops[at, :] = jnp.broadcast_to(top, (rows, LANES))
        totals[at, :] = jnp.broadcast_to(weight, (rows, LANES))
        weights.append((pc.astype(BF16), pf.astype(BF16)))
    for r, at in enumerate(ats):
        o = mm(weights[r][0], values[r]) + mm(weights[r][1], v)
        for i in range(KW // LANES):
            o_rows[i, at, :] = o[:, i * LANES : (i + 1) * LANES]

    top = jnp.zeros((count, LANES), F32)
    weight = jnp.zeros((count, LANES), F32)
    for first in range(0, HEADS, per):
        heads = range(first, first + per)
        blocks = [
            move(o_rows[h // GROUP // per, pl.ds(h, count, stride=HEADS), :], h // GROUP, h)
            for h in heads
        ]
        block = blocks[0]
        for i in range(1, per):
            block = jnp.where(lane // HEAD_SIZE == i, blocks[i], block)
        packed[:, column(first)] = block.astype(BF16)
        for h in heads:
            top = jnp.where(lane == h, tops[pl.ds(h, count, stride=HEADS), :], top)
            weight = jnp.where(lane == h, totals[pl.ds(h, count, stride=HEADS), :], weight)
    packed[:, QW:] = sum(
        pltpu.roll(part, i * HEADS, 1) if i else part
        for i, part in enumerate((*split(top), *split(weight)))
    ).astype(BF16)


def read_stats(block):
    block = block.astype(F32)
    both = block + pltpu.roll(block, LANES - HEADS, 1)
    return both, pltpu.roll(both, LANES - 2 * HEADS, 1)


def pack_factors(factor):
    lane = lane_iota(factor.shape)
    high, low = split(factor)
    low = pltpu.roll(low, HEADS, 1)
    return jnp.where(lane < HEADS, high, jnp.where(lane < 2 * HEADS, low, 0.0)).astype(BF16)


def output_kernel(parts, spread, weight, *refs):
    blocks, out = refs[:parts], refs[parts]
    stats = [read_stats(block[:, QW:]) for block in blocks]
    top = functools.reduce(jnp.maximum, [stat[0] for stat in stats])
    factors = [jnp.exp(stat[0] - top) for stat in stats]
    total = sum(stat[1] * factor for stat, factor in zip(stats, factors))
    inverse = 1.0 / jnp.where(lane_iota(top.shape) < HEADS, total, 1.0)
    count = out.shape[0]
    packed = jnp.concatenate([pack_factors(factor * inverse) for factor in factors], axis=0)
    wide = []
    for tile in range(0, QW, TILE):
        at = slice(tile, tile + TILE)
        spreads = mm(packed, spread[:, at])
        wide.append(
            sum(
                spreads[i * count : (i + 1) * count] * block[:, at].astype(F32)
                for i, block in enumerate(blocks)
            ).astype(BF16)
        )
    out[...] = mm(jnp.concatenate(wide, axis=1), weight[...])


def gate_kernel(parts, gains, w_gate, w_up, *refs):
    blocks, (out, rows_ref) = refs[:parts], refs[parts:]
    count = blocks[0].shape[0]
    for i, block in enumerate(blocks):
        rows_ref[i * count : (i + 1) * count, :] = block[...]
    z = here()[1]
    chunks, size = out.shape[0], out.shape[1]
    taken = [
        rows_ref[pl.ds(pl.multiple_of((z ^ j) * size, size), size), :].astype(F32)
        for j in range(chunks)
    ]
    x = jnp.concatenate(taken, axis=0)
    squares = jnp.sum(x * x, axis=-1, keepdims=True)
    scaled = (x * gains[...].astype(F32)).astype(BF16)
    hid = w_gate.shape[1]
    tile = min(TILE, hid)
    for base, weight in ((0, w_gate), (hid, w_up)):
        for start in range(0, hid, tile):
            terms = mm(scaled, weight[:, start : start + tile]).astype(BF16)
            for j in range(chunks):
                out[j, :, base + start : base + start + tile] = terms[j * size : (j + 1) * size]
    tail = tail_of(squares).astype(BF16)
    for j in range(chunks):
        out[j, :, 2 * hid :] = tail[j * size : (j + 1) * size]


def hidden_kernel(parts, *refs):
    blocks, out = refs[:parts], refs[parts]
    hid = out.shape[1]
    total = blocks[0][:, : 2 * hid].astype(F32)
    for block in blocks[1:]:
        total = total + block[:, : 2 * hid].astype(F32)
    squares = tail_sum(*[block[:, 2 * hid :] for block in blocks])
    inverse = lax.rsqrt(squares / D + EPSILON)
    gate, up = total[:, :hid] * inverse, total[:, hid:] * inverse
    out[...] = (gate / (1.0 + jnp.exp(-gate)) * up).astype(BF16)


def down_kernel(parts, w_down, *refs):
    mine, theirs, (out, rows_ref) = refs[:parts], refs[parts : 2 * parts], refs[2 * parts :]
    core, z = here()[:2]
    size, hid = mine[0].shape
    near = jnp.concatenate([ref[...] for ref in mine], axis=0)
    far = jnp.concatenate([ref[...] for ref in theirs], axis=0)
    total = mm(near, w_down[pl.ds(pl.multiple_of(core * hid, hid), hid), :]) + mm(
        far, w_down[pl.ds(pl.multiple_of((1 - core) * hid, hid), hid), :]
    )
    for j in range(parts):
        rows_ref[pl.ds(pl.multiple_of((z ^ j) * size, size), size), :] = total[
            j * size : (j + 1) * size
        ]
    count = out.shape[1]
    for k in range(out.shape[0]):
        out[k] = rows_ref[k * count : (k + 1) * count, :].astype(BF16)


def shards(
    seq_size,
    req_size,
    token_ids,
    embed_table,
    cache_len,
    range_start,
    positions,
    cached_key_rows,
    cached_value_rows,
    attn_gain,
    mlp_gain,
    w_qkv,
    w_out,
    w_gate,
    w_up,
    w_down,
):
    requests, steps = cache_len.shape[0], token_ids.shape[1]
    count = requests * steps
    feat = embed_table.shape[1]
    core = lax.axis_index("seq") % 2
    depth = seq_size // 2
    swap = lambda array: exchange(array, "seq", seq_size, 1)
    over_z = lambda array, mask: exchange(array, "seq", seq_size, 2 * mask)
    over_req = lambda array, mask: exchange(array, "req", req_size, mask)

    rows = 16
    found = call(
        functools.partial(lookup_kernel, rows),
        shape((req_size, count, feat), BF16),
        (token_ids.T, embed_table),
        [SMEM, HBM],
        [
            pltpu.VMEM((req_size * count, rows, feat), BF16),
            pltpu.VMEM((req_size * count + 8, feat), F32),
            pltpu.SMEM((2, req_size * count + 1), jnp.int32),
            pltpu.SemaphoreType.DMA,
        ],
        limit=LOOKUP_LIMIT,
        name="lookup",
    )
    blocks = direct([found[k] for k in range(req_size)], req_size, over_req, REQ_ORDER)
    hid = w_gate.shape[1] // 2
    context = cached_key_rows.shape[1]
    when = (positions[:, None] + jnp.arange(steps, dtype=jnp.int32)[None, :]).astype(F32)
    cosine, sine, bias = call(
        tables_kernel,
        (shape((count, LANES), F32),) * 2 + (shape((requests, 2 * context), F32),),
        (range_start, cache_len, when.reshape(count, 1)),
        [SMEM, SMEM, VMEM],
        cost=work(1 << 20),
        name="tables",
    )
    *blocks, cosine, sine, bias = lax.optimization_barrier((*blocks, cosine, sine, bias))

    keys2, values2 = swap(cached_key_rows), swap(cached_value_rows)
    *blocks, keys2, values2 = lax.optimization_barrier((*blocks, keys2, values2))
    next_gain = mlp_gain.reshape(1, feat)

    x, keep, give = call(
        functools.partial(project_kernel, req_size),
        (
            shape((count, feat), BF16),
            shape((count, WIDE), BF16),
            shape((count, WIDE + 2 * feat), BF16),
        ),
        (attn_gain.reshape(1, feat), next_gain, w_qkv, *blocks),
        [VMEM] * (3 + req_size),
        name="project",
    )
    got = swap(give)
    mine = call(add_kernel, shape((count, WIDE), BF16), (keep, got), [VMEM] * 2, name="add")
    sums = direct(mine, depth, over_z, WIDE_ORDER)
    _, w_gate, w_out = lax.optimization_barrier((mine, w_gate, w_out))
    gate2, out2 = swap(w_gate), swap(w_out)
    keys, values = call(
        stage_cache_kernel,
        (shape((requests, 2 * context, KW), BF16),) * 2,
        (cached_key_rows, keys2, cached_value_rows, values2),
        [HBM] * 4,
        [pltpu.SemaphoreType.DMA((4 * requests,))],
        cost=time_of(8 * requests * context * KW * 2),
        limit=STAGE_LIMIT,
        name="stage_cache",
    )
    *sums, keys, values, gate2, out2 = lax.optimization_barrier((*sums, keys, values, gate2, out2))

    spread = jnp.asarray(
        (np.arange(LANES)[:, None] % HEADS == np.arange(QW)[None, :] // HEAD_SIZE)
        & (np.arange(LANES)[:, None] < 2 * HEADS),
        BF16,
    )
    packed_width = QW + LANES
    packed, new_k, new_v = call(
        functools.partial(attend_kernel, steps, len(sums)),
        (shape((count, packed_width), BF16), shape((count, KW), BF16), shape((count, KW), BF16)),
        (cosine, sine, bias, keys, values, *sums),
        [VMEM] * (5 + len(sums)),
        [pltpu.VMEM((KW // LANES, count * HEADS, LANES), F32)] * 2
        + [pltpu.VMEM((count * HEADS, LANES), F32)] * 2,
        name="attend",
    )
    partials = direct(packed, depth, over_z, NARROW_ORDER)
    o_pair = call(
        stage_out_kernel,
        shape((QW, 2 * feat), BF16),
        (w_out, out2),
        [HBM] * 2,
        [pltpu.SemaphoreType.DMA((8,))],
        cost=work(4 * feat * QW * 2),
        limit=STAGE_LIMIT,
        name="stage_out",
    )
    def stage_units(own, two):
        return call(
            stage_units_kernel,
            shape((2 * feat, hid), BF16),
            (own, two),
            [HBM] * 2,
            [pltpu.SemaphoreType.DMA((16,))],
            cost=work(4 * feat * hid * 2),
            limit=STAGE_LIMIT,
            name="stage_units",
        )

    _, w_up = lax.optimization_barrier((packed, w_up))
    up2 = swap(w_up)
    g_pair = stage_units(w_gate, gate2)
    *partials, o_pair, g_pair, up2 = lax.optimization_barrier((*partials, o_pair, g_pair, up2))
    part = call(
        functools.partial(output_kernel, depth),
        shape((count, 2 * feat), F32),
        (spread, o_pair, *partials),
        [VMEM] * (2 + depth),
        name="output",
    )
    pair = lambda own, two: jnp.where(
        core == 0, jnp.concatenate([own, two], axis=1), jnp.concatenate([two, own], axis=1)
    )
    x_pair = pair(x, got[:, WIDE : WIDE + feat])
    gain_pair = pair(next_gain, got[0:1, WIDE + feat :])
    resid = (x_pair.astype(F32) + (part + swap(part))).astype(BF16)

    _, new_k, new_v = lax.optimization_barrier((part, new_k, new_v))
    kv_two = swap(jnp.concatenate([new_k, new_v], axis=1))
    taken = direct(resid, req_size, over_req, REQ_ORDER)
    u_pair = stage_units(w_up, up2)
    *taken, u_pair = lax.optimization_barrier((*taken, u_pair))
    size = req_size * count // depth
    terms = call(
        functools.partial(gate_kernel, req_size),
        shape((depth, size, 2 * hid + LANES), BF16),
        (gain_pair, g_pair, u_pair, *taken),
        [VMEM] * (3 + req_size),
        [pltpu.VMEM((req_size * count, 2 * feat), BF16)],
        name="gate",
    )
    sums = direct([terms[j] for j in range(depth)], depth, over_z, WIDE_ORDER)
    all_k, all_v = call(
        join_kernel,
        (shape((requests, steps, 2 * KW), BF16),) * 2,
        (new_k, new_v, kv_two),
        [VMEM] * 3,
        cost=work(1 << 20),
        name="join",
    )
    *sums, all_k, all_v = lax.optimization_barrier((*sums, all_k, all_v))
    hidden = call(
        functools.partial(hidden_kernel, depth),
        shape((size, hid), BF16),
        sums,
        [VMEM] * depth,
        name="hidden",
    )
    near = direct(hidden, depth, over_z, NARROW_ORDER)
    far = [swap(block) for block in near]
    back = call(
        functools.partial(down_kernel, depth),
        shape((req_size, count, feat), BF16),
        (w_down, *near, *far),
        [VMEM] * (1 + 2 * depth),
        [pltpu.VMEM((req_size * count, feat), F32)],
        name="down",
    )
    total = sum(
        block.astype(F32)
        for block in direct([back[k] for k in range(req_size)], req_size, over_req, REQ_ORDER)
    )
    resid_own = lax.dynamic_slice_in_dim(resid, core * feat, feat, axis=1)
    layer_out = (resid_own.astype(F32) + total).astype(BF16).reshape(requests, steps, feat)
    return layer_out, all_k, all_v


def solution(mesh):
    in_specs = (
        P(),
        P("req", "seq"),
        P("req"),
        P("req"),
        P("req"),
        P("req", "seq", None),
        P("req", "seq", None),
        P("seq"),
        P("seq"),
        P("seq", None),
        P(None, "seq"),
        P("seq", "req"),
        P("seq", "req"),
        P("req", "seq"),
    )
    out_specs = (P("req", None, "seq"), P("req", None, None), P("req", None, None))
    body = functools.partial(shards, mesh.shape["seq"], mesh.shape["req"])
    return jax.shard_map(body, mesh=mesh, in_specs=in_specs, out_specs=out_specs, check_vma=False)
```
